256 devices in a mesh: layer: 64 (over y, x, z_lo, core), batch: 4 (over z_hi).
Axes of the slice: x: 4, y: 4, z: 8 (z_hi: 4, z_lo: 2; z = z_hi * 2 + z_lo), core: 2. Of those that a mesh axis runs over, the one named last changes fastest.
Arguments:
- images: bfloat16 [32, 4, 4, 512], P('batch'), parts along dimension 0, may hold values from -6 to 6
- weights: bfloat16 [128, 4608, 512], P('layer'), may hold values from -0.25 to 0.25
- biases: float32 [128, 512], P('layer'), may hold values from -3 to 3
Outputs:
- states: float32 [128, 32, 4, 4, 512], P('layer', 'batch'), parts along dimension 1
The draws below stay inside these ranges and needn't reach their ends.
There are 4 independent parts, one for each index of `batch`. The reference program is written for one: setup_inputs(seed, part) draws one part's arguments, and reference() takes and returns one part's arrays. A program takes and returns all parts, laid end to end along the dimension named above; an argument that names none is the same for every part. Nothing has to cross between parts.
All inputs are finite; a program needn't handle non-finite values.
Results may differ from the reference program's by a relative error of at most 0.015.
Values sent between devices are 32-bit elements; how exact they have to be, the bound alone decides.
No kernel may reach another device: no remote copies, remote signals or barrier semaphores. Data moves between devices by JAX's collectives and lax.ppermute only.
A program may use at most 64 MiB of HBM per device.

```python
import jax
import jax.numpy as jnp
from jax import lax

C = 512
MAP = 4
IMG = 8
LAYERS = 128


def level_of(own_key, dims, shards, low, largest):
    def one(axis_at, parts):
        draws = jax.random.uniform(jax.random.fold_in(jax.random.fold_in(own_key, 6), axis_at), (parts,), jnp.float32, low / len(shards), largest / len(shards))
        return jnp.repeat(jnp.exp(draws), dims[axis_at] // parts).reshape((-1,) + (1,) * (len(dims) - axis_at - 1))

    factor_of = one(*shards[0])
    for cut in shards[1:]:
        factor_of = factor_of * one(*cut)
    return factor_of


def bell_draw(rng, dims, spread, most, cuts=(), held_as=jnp.bfloat16):
    array = spread * jax.random.normal(rng, dims, jnp.float32)
    if cuts:
        array = array * level_of(rng, dims, cuts, -0.22, 0.18)
    return jnp.clip(array, -most, most).astype(held_as)


def setup_inputs(seed: int = 0, part: int = 0) -> dict:
    keys = jax.random.split(jax.random.key(seed), 4)
    part_splits = jax.random.split(jax.random.fold_in(keys[3], part), 4)
    images = bell_draw(part_splits[0], (IMG, MAP, MAP, C), 1.0, 6.0)
    weights = bell_draw(keys[1], (LAYERS, 9 * C, C), C ** -0.5, 0.25, ((0, 64),))
    biases = bell_draw(keys[2], (LAYERS, C), 0.5, 3.0, ((0, 64),), jnp.float32)
    return {"images": images, "weights": weights, "biases": biases}


step_size = 0.25


def fine_step(field, weight, bias):
    channels = field.shape[-1]
    height = field.shape[1]
    breadth = field.shape[2]
    lowered = field.astype(jnp.bfloat16)
    padded = jnp.pad(lowered, ((0, 0), (1, 1), (1, 1), (0, 0)))
    pieces = [padded[:, row_shift:row_shift + height, col_shift:col_shift + breadth, :] for row_shift in range(3) for col_shift in range(3)]
    stacked = jnp.concatenate(pieces, axis=-1).reshape(-1, 9 * channels)
    mixed = jnp.dot(stacked, weight, preferred_element_type=jnp.float32).reshape(field.shape) + bias
    return field + step_size * jnp.tanh(mixed)


def coarse_step(field, weight, bias):
    channels = field.shape[-1]
    lowered = field.astype(jnp.bfloat16).reshape(-1, channels)
    centre = weight[4 * channels:5 * channels]
    mixed = jnp.dot(lowered, centre, preferred_element_type=jnp.float32).reshape(field.shape) + bias
    return field + 2.0 * step_size * jnp.tanh(mixed)


def reference(images, weights, biases):
    channels = images.shape[-1]
    blocks = weights.shape[0] // 2
    block_weights = weights.reshape(blocks, 2, 9 * channels, channels)
    block_biases = biases.reshape(blocks, 2, channels)
    initial = images.astype(jnp.float32)

    def relax_block(pair):
        kernel, offset_bias = pair
        return fine_step(fine_step(initial, kernel[0], offset_bias[0]), kernel[1], offset_bias[1])

    guessed = lax.map(relax_block, (block_weights, block_biases))
    shifted = jnp.concatenate([initial[None], guessed[:-1]], axis=0)

    def forcing_block(triple):
        begin, kernel, offset_bias = triple
        relaxed = fine_step(begin, kernel[0], offset_bias[0])
        return fine_step(relaxed, kernel[1], offset_bias[1]) - coarse_step(begin, kernel[0], offset_bias[0])

    forcing = lax.map(forcing_block, (shifted, block_weights, block_biases))

    def chain_step(current, triple):
        extra, kernel, offset_bias = triple
        following = coarse_step(current, kernel[0], offset_bias[0]) + extra
        return following, following

    _, coarse = lax.scan(chain_step, initial, (forcing, block_weights, block_biases))
    predecessors = jnp.concatenate([initial[None], coarse[:-1]], axis=0)

    def finish_block(triple):
        begin, kernel, offset_bias = triple
        return fine_step(begin, kernel[0], offset_bias[0])

    finished = lax.map(finish_block, (predecessors, block_weights, block_biases))
    states = jnp.stack([finished, coarse], axis=1)
    return states.reshape((weights.shape[0],) + initial.shape)
```

```python
import functools

import jax
import jax.numpy as jnp
from jax import lax
from jax.experimental import pallas as pl
from jax.experimental.pallas import tpu as pltpu
from jax.sharding import PartitionSpec as P

step_size = 0.25
GROUP = 8
PAD = 8


def fine_step(field, weight, bias):
    channels = field.shape[-1]
    height = field.shape[1]
    breadth = field.shape[2]
    lowered = field.astype(jnp.bfloat16)
    padded = jnp.pad(lowered, ((0, 0), (1, 1), (1, 1), (0, 0)))
    pieces = [
        padded[:, row_shift : row_shift + height, col_shift : col_shift + breadth, :]
        for row_shift in range(3)
        for col_shift in range(3)
    ]
    stacked = jnp.concatenate(pieces, axis=-1).reshape(-1, 9 * channels)
    mixed = jnp.dot(stacked, weight, preferred_element_type=jnp.float32).reshape(field.shape) + bias
    return field + step_size * jnp.tanh(mixed)


def coarse_step(field, weight, bias):
    channels = field.shape[-1]
    lowered = field.astype(jnp.bfloat16).reshape(-1, channels)
    centre = weight[4 * channels : 5 * channels]
    mixed = jnp.dot(lowered, centre, preferred_element_type=jnp.float32).reshape(field.shape) + bias
    return field + 2.0 * step_size * jnp.tanh(mixed)


def lower_kernel(*refs):
    out = refs[-1]
    halves = refs[:-1]
    for n, ref in enumerate(halves):
        rows = ref.shape[0]
        slot, part = divmod(n * rows, out.shape[1])
        out[slot, part : part + rows] = ref[...].astype(jnp.bfloat16)


def chain_kernel(turn, spots, state, centres, extras, starts_in, starts, end):
    del starts_in
    rows = state.shape[0]

    @pl.when(spots[0] == turn)
    def _():
        mine = spots[1]
        current = state[...]
        for at in range(GROUP):
            starts[at] = current
            mixed = jnp.dot(
                current.astype(jnp.bfloat16),
                centres[lax.bitwise_xor(mine, at)],
                preferred_element_type=jnp.float32,
            )
            bias = extras[at, rows : rows + 1]
            current = current + 2.0 * step_size * jnp.tanh(mixed + bias) + extras[at, :rows]
        end[...] = current


def solution(mesh):
    blocks = mesh.shape["layer"]
    parts = mesh.shape["batch"]
    groups = blocks // GROUP
    both = ("layer", "batch")

    def route(step):
        pairs = []
        for block in range(blocks):
            for part in range(parts):
                there, other = step(block, part)
                pairs.append((block * parts + part, there * parts + other))
        return pairs

    def upward(block, part):
        return block ^ 2, (part + ((block >> 1) & 1)) % parts

    def downward(block, part):
        return block ^ 2, (part + ((block >> 1) & 1) - 1) % parts

    up, down = route(upward), route(downward)
    beside = route(lambda block, part: (block ^ 4, part))
    twin = route(lambda block, part: (block ^ 1, part))

    def across(pair_of_halves):
        top, bottom = pair_of_halves
        return lax.ppermute(top, both, up), lax.ppermute(bottom, both, down)

    def swap(pair_of_halves, pairs):
        return tuple(lax.ppermute(half, both, pairs) for half in pair_of_halves)

    def shards(images, weights, biases):
        channels = images.shape[-1]
        position = lax.axis_index("layer")
        is_head = position == 0
        mine = position % GROUP
        spots = jnp.stack([position // GROUP, mine]).astype(jnp.int32)
        initial = images.astype(jnp.float32)
        cells = initial.shape[0] * initial.shape[1] * initial.shape[2]
        rows = cells // GROUP

        centre = weights[0, 4 * channels : 5 * channels].astype(jnp.float32)
        slots = [None] * GROUP
        slots[0] = (centre[: channels // 2], centre[channels // 2 :])
        slots[2] = across(slots[0])
        slots[4] = swap(slots[0], beside)
        slots[6] = across(slots[4])
        for at in range(0, GROUP, 2):
            slots[at + 1] = swap(slots[at], twin)

        guessed = fine_step(fine_step(initial, weights[0], biases[0]), weights[1], biases[1])
        incoming = lax.ppermute(guessed, "layer", [(i, i + 1) for i in range(blocks - 1)])
        shifted = jnp.where(is_head, initial, incoming)
        relaxed = fine_step(shifted, weights[0], biases[0])
        forcing = fine_step(relaxed, weights[1], biases[1]) - coarse_step(
            shifted, weights[0], biases[0]
        )
        teams = [[g * GROUP + i for i in range(GROUP)] for g in range(groups)]
        packed = jnp.concatenate(
            [
                forcing.reshape(GROUP, rows, channels),
                jnp.broadcast_to(biases[0], (GROUP, PAD, channels)),
            ],
            axis=1,
        )
        extras = lax.all_to_all(packed, "layer", 0, 0, axis_index_groups=teams)

        vmem = pl.BlockSpec(memory_space=pltpu.VMEM)
        smem = pl.BlockSpec(memory_space=pltpu.SMEM)
        centres = pl.pallas_call(
            lower_kernel,
            out_shape=jax.ShapeDtypeStruct((GROUP, channels, channels), jnp.bfloat16),
            in_specs=[vmem] * (2 * GROUP),
            out_specs=vmem,
            compiler_params=pltpu.CompilerParams(vmem_limit_bytes=32 << 20),
        )(*[half for slot in slots for half in slot])

        starts = jnp.zeros((GROUP, rows, channels), jnp.float32)
        state = lax.dynamic_slice_in_dim(initial.reshape(cells, channels), mine * rows, rows)
        for turn in range(groups):
            if turn:
                pairs = [((turn - 1) * GROUP + i, turn * GROUP + i) for i in range(GROUP)]
                state = lax.ppermute(state, "layer", pairs)
            starts, state = pl.pallas_call(
                functools.partial(chain_kernel, turn),
                out_shape=(
                    jax.ShapeDtypeStruct((GROUP, rows, channels), jnp.float32),
                    jax.ShapeDtypeStruct((rows, channels), jnp.float32),
                ),
                in_specs=[smem] + [vmem] * 4,
                out_specs=(vmem, vmem),
                input_output_aliases={4: 0},
                compiler_params=pltpu.CompilerParams(vmem_limit_bytes=32 << 20),
            )(spots, state, centres, extras, starts)

        predecessors = lax.all_to_all(starts, "layer", 0, 0, axis_index_groups=teams)
        predecessors = predecessors.reshape(initial.shape)
        solved = coarse_step(predecessors, weights[0], biases[0]) + forcing
        finished = fine_step(predecessors, weights[0], biases[0])
        return jnp.stack([finished, solved], axis=0)

    return jax.shard_map(
        shards,
        mesh=mesh,
        in_specs=(P("batch", None, None, None), P("layer", None, None), P("layer", None)),
        out_specs=P("layer", "batch", None, None, None),
        check_vma=False,
    )
```

```python
import functools

import jax
import jax.numpy as jnp
from jax import lax
from jax.experimental import pallas as pl
from jax.experimental.pallas import tpu as pltpu
from jax.sharding import PartitionSpec as P

step_size = 0.25
GROUP = 8
PAD = 8
FLIPS = (0, 5, 0, 5, 4, 1, 4, 1)
SIDE = 4
IMAGES = 8
LANES = 128
MIB = 1 << 20

VMEM = pl.BlockSpec(memory_space=pltpu.VMEM)
ANY = pl.BlockSpec(memory_space=pl.ANY)
HBM = pl.BlockSpec(memory_space=pltpu.HBM)


def call(kernel, out_shape, operands, scratch=(), limit=8, flops=0, aliases=None, specs=None, out_specs=None):
    single = not isinstance(out_shape, (tuple, list))
    results = (out_shape,) if single else out_shape
    return pl.pallas_call(
        kernel,
        out_shape=out_shape,
        in_specs=specs or [VMEM] * len(operands),
        out_specs=out_specs or (VMEM if single else [VMEM for _ in out_shape]),
        scratch_shapes=list(scratch),
        input_output_aliases=aliases or {},
        compiler_params=pltpu.CompilerParams(vmem_limit_bytes=limit * MIB),
        cost_estimate=pl.CostEstimate(flops=0, bytes_accessed=0, transcendentals=0),
    )(*operands)


def f32(*shape):
    return jax.ShapeDtypeStruct(shape, jnp.float32)


def spread(field, columns):
    channels = field.shape[-1]
    cells = [field[IMAGES * at : IMAGES * (at + 1)] for at in range(SIDE * SIDE)]
    nothing = jnp.zeros_like(cells[0])
    for tap in range(9):
        down, right = tap // 3 - 1, tap % 3 - 1
        pieces = []
        for row in range(SIDE):
            for col in range(SIDE):
                inside = 0 <= row + down < SIDE and 0 <= col + right < SIDE
                pieces.append(cells[(row + down) * SIDE + col + right] if inside else nothing)
        columns[:, tap * channels : (tap + 1) * channels] = jnp.concatenate(pieces, axis=0).astype(
            jnp.bfloat16
        )


def fine(field, weights, biases, layer, columns):
    spread(field, columns)
    mixed = jnp.dot(columns[...], weights[layer], preferred_element_type=jnp.float32)
    return field + step_size * jnp.tanh(mixed + biases[layer : layer + 1])


def coarse(field, centre, bias):
    mixed = jnp.dot(field.astype(jnp.bfloat16), centre, preferred_element_type=jnp.float32)
    return field + 2.0 * step_size * jnp.tanh(mixed + bias)


def flip_of(position):
    group = lax.div(position, GROUP)
    other_x = lax.bitwise_and(lax.bitwise_xor(group, lax.div(group, 4)), 1)
    return lax.bitwise_or(4 * other_x, lax.bitwise_and(group, 1))


def centre_kernel(weights, biases, whole, landing, sem):
    channels = whole.shape[1]
    copy = pltpu.make_async_copy(weights.at[0, pl.ds(4 * channels, channels)], landing, sem)
    copy.start()
    whole[channels:] = jnp.broadcast_to(biases[0:1], (PAD, channels))
    copy.wait()
    whole[:channels] = landing[...].astype(jnp.float32)


def guess_kernel(initial, weights, biases, guessed, columns):
    first = fine(initial[...], weights, biases, 0, columns)
    guessed[...] = fine(first, weights, biases, 1, columns)


def force_kernel(incoming, initial, weights, biases, packed, columns):
    position = lax.axis_index("layer")
    rows, channels = packed.shape[1:]
    begin = jnp.where(position == 0, initial[...], incoming[...])
    relaxed = fine(begin, weights, biases, 0, columns)
    after = fine(relaxed, weights, biases, 1, columns)
    forcing = after - coarse(
        begin, weights[0, 4 * channels : 5 * channels], biases[0:1]
    )
    flip = flip_of(position)
    for lane in range(GROUP):
        spot = lax.bitwise_xor(flip, lane)
        packed[spot] = forcing[lane * rows : (lane + 1) * rows]


def hold_kernel(*refs):
    del refs


def lower_kernel(begin, count, *refs):
    centres, offsets = refs[-2:]
    channels = centres.shape[1]
    for n in range(count):
        centres[begin + n] = refs[n][:channels].astype(jnp.bfloat16)
        offsets[begin + n] = refs[n][channels:]


def chain_kernel(turn, state, near, near_bias, far, far_bias, extras, *refs):
    starts, end = refs[-2:]
    rows = end.shape[0]
    position = lax.axis_index("layer")
    mine = lax.rem(position, GROUP)

    def walk(order):
        if turn:
            current = state[...]
        else:
            current = state[pl.ds(pl.multiple_of(mine * rows, rows), rows)]
        for at in range(GROUP):
            starts[at] = current
            centres, offsets = order[at // 4]
            slot = lax.bitwise_and(lax.bitwise_xor(mine, at), 3)
            current = coarse(current, centres[slot], offsets[slot, 0:1]) + extras[at]
        end[...] = current

    first, second = (near, near_bias), (far, far_bias)
    here = lax.div(position, GROUP) == turn
    pl.when(here & (mine < 4))(lambda: walk((first, second)))
    pl.when(here & (mine >= 4))(lambda: walk((second, first)))


def finish_kernel(arrived, packed, weights, biases, states, columns, whole):
    position = lax.axis_index("layer")
    channels = arrived.shape[2]
    flip = flip_of(position)
    begin = jnp.concatenate([arrived[lax.bitwise_xor(flip, lane)] for lane in range(GROUP)], axis=0)
    forcing = jnp.concatenate(
        [packed[lax.bitwise_xor(flip, lane)] for lane in range(GROUP)], axis=0
    )
    solved = coarse(begin, weights[0, 4 * channels : 5 * channels], biases[0:1]) + forcing
    finished = fine(begin, weights, biases, 0, columns)
    for layer, value in ((1, solved), (0, finished)):
        for band in range(channels // LANES):
            across = slice(band * LANES, (band + 1) * LANES)
            whole[layer, band] = value[:, across]
            for image in range(IMAGES):
                for row in range(SIDE):
                    states[layer, image, row, :, across] = whole[
                        layer, band, pl.ds(row * SIDE * IMAGES + image, SIDE, stride=IMAGES), :
                    ]


def solution(mesh):
    blocks = mesh.shape["layer"]
    parts = mesh.shape["batch"]
    groups = blocks // GROUP
    both = ("layer", "batch")

    def route(step):
        pairs = []
        for block in range(blocks):
            for part in range(parts):
                there, other = step(block, part)
                pairs.append((block * parts + part, there * parts + other))
        return pairs

    def over(block, part):
        return block ^ 2, (part + ((block >> 1) & 1) - (block & 1)) % parts

    behind = route(over)
    beside = route(lambda block, part: (block ^ 4, part))
    twin = route(lambda block, part: (block ^ 1, part))

    def shards(images, weights, biases):
        channels = images.shape[-1]
        cells = IMAGES * SIDE * SIDE
        rows = cells // GROUP
        columns = pltpu.VMEM((cells, 9 * channels), jnp.bfloat16)
        conv = 2 * cells * 9 * channels * channels

        own = call(
            centre_kernel,
            pltpu.VMEM((channels + PAD, channels), jnp.float32),
            (pltpu.with_memory_space_constraint(weights, pltpu.HBM), biases),
            scratch=[pltpu.VMEM((channels, channels), jnp.bfloat16), pltpu.SemaphoreType.DMA],
            specs=[HBM, VMEM],
        )
        beside_x = lax.ppermute(own, both, beside)
        behind_z = lax.ppermute(own, both, behind)

        initial = images.astype(jnp.float32).reshape(IMAGES, SIDE * SIDE, channels)
        initial = jnp.transpose(initial, (1, 0, 2)).reshape(cells, channels)
        guessed = call(
            guess_kernel, f32(cells, channels), (initial, weights, biases), [columns], flops=2 * conv
        )
        incoming = lax.ppermute(guessed, "layer", [(i, i + 1) for i in range(blocks - 1)])
        packed = call(
            force_kernel,
            f32(GROUP, rows, channels),
            (incoming, initial, weights, biases),
            [columns],
            flops=2 * conv,
        )
        teams = [[g * GROUP + i for i in range(GROUP)] for g in range(groups)]
        extras = lax.all_to_all(packed, "layer", 0, 0, axis_index_groups=teams)

        def hold(each, *after):
            return call(
                hold_kernel,
                f32(*each.shape),
                (each, *after),
                specs=[ANY] * (1 + len(after)),
                out_specs=ANY,
                aliases={0: 0},
            )

        def lowered(begin, pieces, held=()):
            return call(
                functools.partial(lower_kernel, begin, len(pieces)),
                (
                    pltpu.VMEM((4, channels, channels), jnp.bfloat16),
                    pltpu.VMEM((4, PAD, channels), jnp.float32),
                ),
                (*pieces, *held),
                aliases={len(pieces) + n: n for n in range(len(held))},
            )

        behind_z = hold(behind_z, packed)
        beside_x = hold(beside_x, packed)
        held = hold(own, extras)
        corner = lax.ppermute(beside_x, both, behind)
        own_twin = lax.ppermute(held, both, twin)
        behind_twin = lax.ppermute(behind_z, both, twin)
        beside_twin = lax.ppermute(beside_x, both, twin)
        near = lowered(0, (held, own_twin, behind_z, behind_twin))
        far = lowered(0, (beside_x, beside_twin))
        corner = hold(corner, near[1])
        far = lowered(2, (corner, lax.ppermute(corner, both, twin)), far)

        state = initial
        starts = None
        for turn in range(groups):
            operands = (state, *near, *far, extras)
            if turn:
                pairs = [
                    (
                        (turn - 1) * GROUP + (lane ^ FLIPS[turn - 1]),
                        turn * GROUP + (lane ^ FLIPS[turn]),
                    )
                    for lane in range(GROUP)
                ]
                state = lax.ppermute(state, "layer", pairs)
                operands = (state, *near, *far, extras, starts)
            starts, state = call(
                functools.partial(chain_kernel, turn),
                (f32(GROUP, rows, channels), f32(rows, channels)),
                operands,
                aliases={6: 0} if turn else None,
            )

        arrived = lax.all_to_all(starts, "layer", 0, 0, axis_index_groups=teams)
        return call(
            finish_kernel,
            f32(2, IMAGES, SIDE, SIDE, channels),
            (arrived, packed, weights, biases),
            [columns, pltpu.VMEM((2, channels // LANES, cells, LANES), jnp.float32)],
            flops=conv,
        )

    return jax.shard_map(
        shards,
        mesh=mesh,
        in_specs=(P("batch", None, None, None), P("layer", None, None), P("layer", None)),
        out_specs=P("layer", "batch", None, None, None),
        check_vma=False,
    )
```

```python
import functools

import jax
import jax.numpy as jnp
from jax import lax
from jax.experimental import pallas as pl
from jax.experimental.pallas import tpu as pltpu
from jax.sharding import PartitionSpec as P

step_size = 0.25
GROUP = 8
PAD = 8
FLIPS = (0, 5, 0, 5, 4, 1, 4, 1)
SIDE = 4
IMAGES = 8
LANES = 128
MIB = 1 << 20

VMEM = pl.BlockSpec(memory_space=pltpu.VMEM)
ANY = pl.BlockSpec(memory_space=pl.ANY)
HBM = pl.BlockSpec(memory_space=pltpu.HBM)


def call(kernel, out_shape, operands, scratch=(), limit=8, flops=0, aliases=None, specs=None, out_specs=None):
    single = not isinstance(out_shape, (tuple, list))
    results = (out_shape,) if single else out_shape
    return pl.pallas_call(
        kernel,
        out_shape=out_shape,
        in_specs=specs or [VMEM] * len(operands),
        out_specs=out_specs or (VMEM if single else [VMEM for _ in out_shape]),
        scratch_shapes=list(scratch),
        input_output_aliases=aliases or {},
        compiler_params=pltpu.CompilerParams(vmem_limit_bytes=limit * MIB),
        cost_estimate=pl.CostEstimate(flops=0, bytes_accessed=0, transcendentals=0),
    )(*operands)


def f32(*shape):
    return jax.ShapeDtypeStruct(shape, jnp.float32)


def spread(field, columns):
    channels = field.shape[-1]
    cells = [field[IMAGES * at : IMAGES * (at + 1)] for at in range(SIDE * SIDE)]
    nothing = jnp.zeros_like(cells[0])
    for tap in range(9):
        down, right = tap // 3 - 1, tap % 3 - 1
        pieces = []
        for row in range(SIDE):
            for col in range(SIDE):
                inside = 0 <= row + down < SIDE and 0 <= col + right < SIDE
                pieces.append(cells[(row + down) * SIDE + col + right] if inside else nothing)
        columns[:, tap * channels : (tap + 1) * channels] = jnp.concatenate(pieces, axis=0).astype(
            jnp.bfloat16
        )


def fine(field, weights, biases, layer, columns):
    spread(field, columns)
    mixed = jnp.dot(columns[...], weights[layer], preferred_element_type=jnp.float32)
    return field + step_size * jnp.tanh(mixed + biases[layer : layer + 1])


def coarse(field, centre, bias):
    mixed = jnp.dot(field.astype(jnp.bfloat16), centre, preferred_element_type=jnp.float32)
    return field + 2.0 * step_size * jnp.tanh(mixed + bias)


def flip_of(position):
    group = lax.div(position, GROUP)
    other_x = lax.bitwise_and(lax.bitwise_xor(group, lax.div(group, 4)), 1)
    return lax.bitwise_or(4 * other_x, lax.bitwise_and(group, 1))


def centre_kernel(weights, biases, whole, landing, offsets, sems):
    channels = whole.shape[1]
    copy = pltpu.make_async_copy(
        weights.at[0, pl.ds(4 * channels, channels)], landing, sems.at[0]
    )
    offset_copy = pltpu.make_async_copy(biases, offsets, sems.at[1])
    copy.start()
    offset_copy.start()
    offset_copy.wait()
    whole[channels:] = jnp.broadcast_to(offsets[0:1], (PAD, channels))
    copy.wait()
    whole[:channels] = landing[...].astype(jnp.float32)


def guess_kernel(initial, weights, biases, guessed, columns):
    first = fine(initial[...], weights, biases, 0, columns)
    guessed[...] = fine(first, weights, biases, 1, columns)


def force_kernel(incoming, initial, weights, biases, packed, columns):
    position = lax.axis_index("layer")
    rows, channels = packed.shape[1:]
    begin = jnp.where(position == 0, initial[...], incoming[...])
    relaxed = fine(begin, weights, biases, 0, columns)
    after = fine(relaxed, weights, biases, 1, columns)
    forcing = after - coarse(
        begin, weights[0, 4 * channels : 5 * channels], biases[0:1]
    )
    flip = flip_of(position)
    for lane in range(GROUP):
        spot = lax.bitwise_xor(flip, lane)
        packed[spot] = forcing[lane * rows : (lane + 1) * rows]


def hold_kernel(*refs):
    del refs


def lower_kernel(begin, count, *refs):
    centres, offsets = refs[-2:]
    channels = centres.shape[1]
    for n in range(count):
        centres[begin + n] = refs[n][:channels].astype(jnp.bfloat16)
        offsets[begin + n] = refs[n][channels:]


def chain_kernel(turn, last, state, near, near_bias, far, far_bias, extras, *refs):
    starts, end = (refs[-1], None) if last else refs[-2:]
    rows = starts.shape[1]
    position = lax.axis_index("layer")
    mine = lax.rem(position, GROUP)

    def walk(order):
        if turn:
            current = state[...]
        else:
            current = state[pl.ds(pl.multiple_of(mine * rows, rows), rows)]
        for at in range(GROUP):
            starts[at] = current
            centres, offsets = order[at // 4]
            slot = lax.bitwise_and(lax.bitwise_xor(mine, at), 3)
            current = coarse(current, centres[slot], offsets[slot, 0:1]) + extras[at]
        if not last:
            end[...] = current

    first, second = (near, near_bias), (far, far_bias)
    here = lax.div(position, GROUP) == turn
    pl.when(here & (mine < 4))(lambda: walk((first, second)))
    pl.when(here & (mine >= 4))(lambda: walk((second, first)))


def finish_kernel(arrived, packed, weights, biases, states, columns, whole):
    position = lax.axis_index("layer")
    channels = arrived.shape[2]
    flip = flip_of(position)
    begin = jnp.concatenate([arrived[lax.bitwise_xor(flip, lane)] for lane in range(GROUP)], axis=0)
    forcing = jnp.concatenate(
        [packed[lax.bitwise_xor(flip, lane)] for lane in range(GROUP)], axis=0
    )
    solved = coarse(begin, weights[0, 4 * channels : 5 * channels], biases[0:1]) + forcing
    finished = fine(begin, weights, biases, 0, columns)
    for layer, value in ((1, solved), (0, finished)):
        for band in range(channels // LANES):
            across = slice(band * LANES, (band + 1) * LANES)
            whole[layer, band] = value[:, across]
            for image in range(IMAGES):
                for row in range(SIDE):
                    states[layer, image, row, :, across] = whole[
                        layer, band, pl.ds(row * SIDE * IMAGES + image, SIDE, stride=IMAGES), :
                    ]


def solution(mesh):
    blocks = mesh.shape["layer"]
    parts = mesh.shape["batch"]
    groups = blocks // GROUP
    both = ("layer", "batch")

    def route(step):
        pairs = []
        for block in range(blocks):
            for part in range(parts):
                there, other = step(block, part)
                pairs.append((block * parts + part, there * parts + other))
        return pairs

    def over(block, part):
        return block ^ 2, (part + ((block >> 1) & 1) - (block & 1)) % parts

    behind = route(over)
    beside = route(lambda block, part: (block ^ 4, part))
    twin = route(lambda block, part: (block ^ 1, part))

    def shards(images, weights, biases):
        channels = images.shape[-1]
        cells = IMAGES * SIDE * SIDE
        rows = cells // GROUP
        columns = pltpu.VMEM((cells, 9 * channels), jnp.bfloat16)
        conv = 2 * cells * 9 * channels * channels

        own = call(
            centre_kernel,
            pltpu.VMEM((channels + PAD, channels), jnp.float32),
            [pltpu.with_memory_space_constraint(each, pltpu.HBM) for each in (weights, biases)],
            scratch=[
                pltpu.VMEM((channels, channels), jnp.bfloat16),
                pltpu.VMEM(biases.shape, jnp.float32),
                pltpu.SemaphoreType.DMA((2,)),
            ],
            specs=[HBM, HBM],
        )
        beside_x = lax.ppermute(own, both, beside)
        behind_z = lax.ppermute(own, both, behind)

        initial = images.astype(jnp.float32).reshape(IMAGES, SIDE * SIDE, channels)
        initial = jnp.transpose(initial, (1, 0, 2)).reshape(cells, channels)
        guessed = call(
            guess_kernel, f32(cells, channels), (initial, weights, biases), [columns], flops=2 * conv
        )
        incoming = lax.ppermute(guessed, "layer", [(i, i + 1) for i in range(blocks - 1)])
        packed = call(
            force_kernel,
            f32(GROUP, rows, channels),
            (incoming, initial, weights, biases),
            [columns],
            flops=2 * conv,
        )
        teams = [[g * GROUP + i for i in range(GROUP)] for g in range(groups)]
        extras = lax.all_to_all(packed, "layer", 0, 0, axis_index_groups=teams)

        def hold(each, *after):
            return call(
                hold_kernel,
                f32(*each.shape),
                (each, *after),
                specs=[ANY] * (1 + len(after)),
                out_specs=ANY,
                aliases={0: 0},
            )

        def lowered(begin, pieces, held=()):
            return call(
                functools.partial(lower_kernel, begin, len(pieces)),
                (
                    pltpu.VMEM((4, channels, channels), jnp.bfloat16),
                    pltpu.VMEM((4, PAD, channels), jnp.float32),
                ),
                (*pieces, *held),
                aliases={len(pieces) + n: n for n in range(len(held))},
            )

        behind_z = hold(behind_z, packed)
        beside_x = hold(beside_x, packed)
        held = hold(own, extras)
        corner = lax.ppermute(beside_x, both, behind)
        own_twin = lax.ppermute(held, both, twin)
        behind_twin = lax.ppermute(behind_z, both, twin)
        beside_twin = lax.ppermute(beside_x, both, twin)
        near = lowered(0, (held, own_twin, behind_z, behind_twin))
        far = lowered(0, (beside_x, beside_twin))
        corner = hold(corner, near[1])
        far = lowered(2, (corner, lax.ppermute(corner, both, twin)), far)

        state = [initial]
        starts = None
        for turn in range(groups):
            operands = (*state, *near, *far, extras)
            if turn:
                pairs = [
                    (
                        (turn - 1) * GROUP + (lane ^ FLIPS[turn - 1]),
                        turn * GROUP + (lane ^ FLIPS[turn]),
                    )
                    for lane in range(GROUP)
                ]
                state = [lax.ppermute(*state, "layer", pairs)]
                operands = (*state, *near, *far, extras, starts)
            last = turn == groups - 1
            starts, *state = call(
                functools.partial(chain_kernel, turn, last),
                [f32(GROUP, rows, channels)] + [f32(rows, channels)] * (not last),
                operands,
                aliases={6: 0} if turn else None,
            )

        arrived = lax.all_to_all(starts, "layer", 0, 0, axis_index_groups=teams)
        return call(
            finish_kernel,
            f32(2, IMAGES, SIDE, SIDE, channels),
            (arrived, packed, weights, biases),
            [columns, pltpu.VMEM((2, channels // LANES, cells, LANES), jnp.float32)],
            flops=conv,
        )

    return jax.shard_map(
        shards,
        mesh=mesh,
        in_specs=(P("batch", None, None, None), P("layer", None, None), P("layer", None)),
        out_specs=P("layer", "batch", None, None, None),
        check_vma=False,
    )
```

```python
import functools

import jax
import jax.numpy as jnp
from jax import lax
from jax.experimental import pallas as pl
from jax.experimental.pallas import tpu as pltpu
from jax.sharding import PartitionSpec as P

step_size = 0.25
GROUP = 8
PAD = 8
CUT = 344
FLIPS = (0, 5, 0, 5, 4, 1, 4, 1)
SIDE = 4
IMAGES = 8
LANES = 128
MIB = 1 << 20

VMEM = pl.BlockSpec(memory_space=pltpu.VMEM)
ANY = pl.BlockSpec(memory_space=pl.ANY)
HBM = pl.BlockSpec(memory_space=pltpu.HBM)


def call(kernel, out_shape, operands, scratch=(), limit=8, flops=0, aliases=None, specs=None, out_specs=None):
    single = not isinstance(out_shape, (tuple, list))
    results = (out_shape,) if single else out_shape
    return pl.pallas_call(
        kernel,
        out_shape=out_shape,
        in_specs=specs or [VMEM] * len(operands),
        out_specs=out_specs or (VMEM if single else [VMEM for _ in out_shape]),
        scratch_shapes=list(scratch),
        input_output_aliases=aliases or {},
        compiler_params=pltpu.CompilerParams(vmem_limit_bytes=limit * MIB),
        cost_estimate=pl.CostEstimate(flops=0, bytes_accessed=0, transcendentals=0),
    )(*operands)


def f32(*shape):
    return jax.ShapeDtypeStruct(shape, jnp.float32)


def spread(field, columns):
    channels = field.shape[-1]
    cells = [field[IMAGES * at : IMAGES * (at + 1)] for at in range(SIDE * SIDE)]
    nothing = jnp.zeros_like(cells[0])
    for tap in range(9):
        down, right = tap // 3 - 1, tap % 3 - 1
        pieces = []
        for row in range(SIDE):
            for col in range(SIDE):
                inside = 0 <= row + down < SIDE and 0 <= col + right < SIDE
                pieces.append(cells[(row + down) * SIDE + col + right] if inside else nothing)
        columns[:, tap * channels : (tap + 1) * channels] = jnp.concatenate(pieces, axis=0).astype(
            jnp.bfloat16
        )


def fine(field, weights, biases, layer, columns):
    spread(field, columns)
    mixed = jnp.dot(columns[...], weights[layer], preferred_element_type=jnp.float32)
    return field + step_size * jnp.tanh(mixed + biases[layer : layer + 1])


def coarse(field, centre, bias):
    mixed = jnp.dot(field.astype(jnp.bfloat16), centre, preferred_element_type=jnp.float32)
    return field + 2.0 * step_size * jnp.tanh(mixed + bias)


def flip_of(position):
    group = lax.div(position, GROUP)
    other_x = lax.bitwise_and(lax.bitwise_xor(group, lax.div(group, 4)), 1)
    return lax.bitwise_or(4 * other_x, lax.bitwise_and(group, 1))


def centre_kernel(weights, biases, whole, landing, offsets, sems):
    channels = whole.shape[1]
    copy = pltpu.make_async_copy(
        weights.at[0, pl.ds(4 * channels, channels)], landing, sems.at[0]
    )
    offset_copy = pltpu.make_async_copy(biases, offsets, sems.at[1])
    copy.start()
    offset_copy.start()
    offset_copy.wait()
    whole[channels:] = jnp.broadcast_to(offsets[0:1], (PAD, channels))
    copy.wait()
    whole[:channels] = landing[...].astype(jnp.float32)


def guess_kernel(initial, weights, biases, guessed, columns):
    first = fine(initial[...], weights, biases, 0, columns)
    guessed[...] = fine(first, weights, biases, 1, columns)


def force_kernel(incoming, initial, weights, biases, packed, columns):
    position = lax.axis_index("layer")
    rows, channels = packed.shape[1:]
    begin = jnp.where(position == 0, initial[...], incoming[...])
    relaxed = fine(begin, weights, biases, 0, columns)
    after = fine(relaxed, weights, biases, 1, columns)
    forcing = after - coarse(
        begin, weights[0, 4 * channels : 5 * channels], biases[0:1]
    )
    flip = flip_of(position)
    for lane in range(GROUP):
        spot = lax.bitwise_xor(flip, lane)
        packed[spot] = forcing[lane * rows : (lane + 1) * rows]


def hold_kernel(*refs):
    del refs


def part_kernel(begin, whole, after, part):
    del after
    part[...] = whole[begin : begin + part.shape[0]]


def lower_kernel(begin, counts, *refs):
    centres, offsets = refs[-2:]
    channels = centres.shape[1]
    at = 0
    for n, count in enumerate(counts):
        spot = 0
        for ref in refs[at : at + count]:
            rows = min(ref.shape[0], channels - spot)
            centres[begin + n, spot : spot + rows] = ref[:rows].astype(jnp.bfloat16)
            spot += rows
        offsets[begin + n] = ref[rows:]
        at += count


def chain_kernel(turn, last, state, near, near_bias, far, far_bias, extras, *refs):
    starts, end = (refs[-1], None) if last else refs[-2:]
    rows = starts.shape[1]
    position = lax.axis_index("layer")
    mine = lax.rem(position, GROUP)

    def walk(order):
        if turn:
            current = state[...]
        else:
            current = state[pl.ds(pl.multiple_of(mine * rows, rows), rows)]
        for at in range(GROUP):
            starts[at] = current
            centres, offsets = order[at // 4]
            slot = lax.bitwise_and(lax.bitwise_xor(mine, at), 3)
            current = coarse(current, centres[slot], offsets[slot, 0:1]) + extras[at]
        if not last:
            end[...] = current

    first, second = (near, near_bias), (far, far_bias)
    here = lax.div(position, GROUP) == turn
    pl.when(here & (mine < 4))(lambda: walk((first, second)))
    pl.when(here & (mine >= 4))(lambda: walk((second, first)))


def finish_kernel(arrived, packed, weights, biases, states, columns, whole):
    position = lax.axis_index("layer")
    channels = arrived.shape[2]
    flip = flip_of(position)
    begin = jnp.concatenate([arrived[lax.bitwise_xor(flip, lane)] for lane in range(GROUP)], axis=0)
    forcing = jnp.concatenate(
        [packed[lax.bitwise_xor(flip, lane)] for lane in range(GROUP)], axis=0
    )
    solved = coarse(begin, weights[0, 4 * channels : 5 * channels], biases[0:1]) + forcing
    finished = fine(begin, weights, biases, 0, columns)
    for layer, value in ((1, solved), (0, finished)):
        for band in range(channels // LANES):
            across = slice(band * LANES, (band + 1) * LANES)
            whole[layer, band] = value[:, across]
            for image in range(IMAGES):
                for row in range(SIDE):
                    states[layer, image, row, :, across] = whole[
                        layer, band, pl.ds(row * SIDE * IMAGES + image, SIDE, stride=IMAGES), :
                    ]


def solution(mesh):
    blocks = mesh.shape["layer"]
    parts = mesh.shape["batch"]
    groups = blocks // GROUP
    both = ("layer", "batch")

    def route(step):
        pairs = []
        for block in range(blocks):
            for part in range(parts):
                there, other = step(block, part)
                pairs.append((block * parts + part, there * parts + other))
        return pairs

    def over(block, part):
        return block ^ 2, (part + ((block >> 1) & 1) - (block & 1)) % parts

    behind = route(over)
    beside = route(lambda block, part: (block ^ 4, part))
    twin = route(lambda block, part: (block ^ 1, part))

    def shards(images, weights, biases):
        channels = images.shape[-1]
        cells = IMAGES * SIDE * SIDE
        rows = cells // GROUP
        columns = pltpu.VMEM((cells, 9 * channels), jnp.bfloat16)
        conv = 2 * cells * 9 * channels * channels

        own = call(
            centre_kernel,
            pltpu.VMEM((channels + PAD, channels), jnp.float32),
            [pltpu.with_memory_space_constraint(each, pltpu.HBM) for each in (weights, biases)],
            scratch=[
                pltpu.VMEM((channels, channels), jnp.bfloat16),
                pltpu.VMEM(biases.shape, jnp.float32),
                pltpu.SemaphoreType.DMA((2,)),
            ],
            specs=[HBM, HBM],
        )
        beside_x = lax.ppermute(own, both, beside)
        behind_z = lax.ppermute(own, both, behind)

        initial = images.astype(jnp.float32).reshape(IMAGES, SIDE * SIDE, channels)
        initial = jnp.transpose(initial, (1, 0, 2)).reshape(cells, channels)
        guessed = call(
            guess_kernel, f32(cells, channels), (initial, weights, biases), [columns], flops=2 * conv
        )
        incoming = lax.ppermute(guessed, "layer", [(i, i + 1) for i in range(blocks - 1)])
        packed = call(
            force_kernel,
            f32(GROUP, rows, channels),
            (incoming, initial, weights, biases),
            [columns],
            flops=2 * conv,
        )
        teams = [[g * GROUP + i for i in range(GROUP)] for g in range(groups)]
        extras = lax.all_to_all(packed, "layer", 0, 0, axis_index_groups=teams)

        def hold(each, *after):
            return call(
                hold_kernel,
                f32(*each.shape),
                (each, *after),
                specs=[ANY] * (1 + len(after)),
                out_specs=ANY,
                aliases={0: 0},
            )

        def lowered(begin, slots, held=()):
            pieces = [each for slot in slots for each in slot]
            return call(
                functools.partial(lower_kernel, begin, [len(slot) for slot in slots]),
                (
                    pltpu.VMEM((4, channels, channels), jnp.bfloat16),
                    pltpu.VMEM((4, PAD, channels), jnp.float32),
                ),
                (*pieces, *held),
                aliases={len(pieces) + n: n for n in range(len(held))},
            )

        def part(whole, begin, end, after):
            return call(
                functools.partial(part_kernel, begin),
                pltpu.VMEM((end - begin, channels), jnp.float32),
                (whole, after),
                specs=[VMEM, ANY],
            )

        behind_z = hold(behind_z, packed)
        beside_x = hold(beside_x, packed)
        held = hold(own, extras)
        corner = [
            lax.ppermute(part(beside_x, 0, CUT, extras), both, behind),
            lax.ppermute(part(behind_z, CUT, channels + PAD, extras), both, beside),
        ]
        own_twin = lax.ppermute(held, both, twin)
        behind_twin = lax.ppermute(behind_z, both, twin)
        beside_twin = lax.ppermute(beside_x, both, twin)
        near = lowered(0, ([held], [own_twin], [behind_z], [behind_twin]))
        far = lowered(0, ([beside_x], [beside_twin]))
        corner = [hold(each, near[1]) for each in corner]
        corner_twin = [lax.ppermute(each, both, twin) for each in corner]
        far = lowered(2, (corner, corner_twin), far)

        state = [initial]
        starts = None
        for turn in range(groups):
            operands = (*state, *near, *far, extras)
            if turn:
                pairs = [
                    (
                        (turn - 1) * GROUP + (lane ^ FLIPS[turn - 1]),
                        turn * GROUP + (lane ^ FLIPS[turn]),
                    )
                    for lane in range(GROUP)
                ]
                state = [lax.ppermute(*state, "layer", pairs)]
                operands = (*state, *near, *far, extras, starts)
            last = turn == groups - 1
            starts, *state = call(
                functools.partial(chain_kernel, turn, last),
                [f32(GROUP, rows, channels)] + [f32(rows, channels)] * (not last),
                operands,
                aliases={6: 0} if turn else None,
            )

        arrived = lax.all_to_all(starts, "layer", 0, 0, axis_index_groups=teams)
        return call(
            finish_kernel,
            f32(2, IMAGES, SIDE, SIDE, channels),
            (arrived, packed, weights, biases),
            [columns, pltpu.VMEM((2, channels // LANES, cells, LANES), jnp.float32)],
            flops=conv,
        )

    return jax.shard_map(
        shards,
        mesh=mesh,
        in_specs=(P("batch", None, None, None), P("layer", None, None), P("layer", None)),
        out_specs=P("layer", "batch", None, None, None),
        check_vma=False,
    )
```

```python
import functools

import jax
import jax.numpy as jnp
from jax import lax
from jax.experimental import pallas as pl
from jax.experimental.pallas import tpu as pltpu
from jax.sharding import PartitionSpec as P

step_size = 0.25
GROUP = 8
PAD = 8
CUT = 344
FLIPS = (0, 5, 0, 5, 4, 1, 4, 1)
SIDE = 4
IMAGES = 8
LANES = 128
MIB = 1 << 20

VMEM = pl.BlockSpec(memory_space=pltpu.VMEM)
ANY = pl.BlockSpec(memory_space=pl.ANY)
HBM = pl.BlockSpec(memory_space=pltpu.HBM)


def call(kernel, out_shape, operands, scratch=(), limit=8, flops=0, aliases=None, specs=None, out_specs=None):
    single = not isinstance(out_shape, (tuple, list))
    results = (out_shape,) if single else out_shape
    return pl.pallas_call(
        kernel,
        out_shape=out_shape,
        in_specs=specs or [VMEM] * len(operands),
        out_specs=out_specs or (VMEM if single else [VMEM for _ in out_shape]),
        scratch_shapes=list(scratch),
        input_output_aliases=aliases or {},
        compiler_params=pltpu.CompilerParams(vmem_limit_bytes=limit * MIB),
        cost_estimate=pl.CostEstimate(flops=0, bytes_accessed=0, transcendentals=0),
    )(*operands)


def f32(*shape):
    return jax.ShapeDtypeStruct(shape, jnp.float32)


def spread(field, columns):
    channels = field.shape[-1]
    cells = [field[IMAGES * at : IMAGES * (at + 1)] for at in range(SIDE * SIDE)]
    nothing = jnp.zeros_like(cells[0])
    for tap in range(9):
        down, right = tap // 3 - 1, tap % 3 - 1
        pieces = []
        for row in range(SIDE):
            for col in range(SIDE):
                inside = 0 <= row + down < SIDE and 0 <= col + right < SIDE
                pieces.append(cells[(row + down) * SIDE + col + right] if inside else nothing)
        columns[:, tap * channels : (tap + 1) * channels] = jnp.concatenate(pieces, axis=0).astype(
            jnp.bfloat16
        )


def fine(field, weights, biases, layer, columns):
    spread(field, columns)
    mixed = jnp.dot(columns[...], weights[layer], preferred_element_type=jnp.float32)
    return field + step_size * jnp.tanh(mixed + biases[layer : layer + 1])


def coarse(field, centre, bias):
    mixed = jnp.dot(field.astype(jnp.bfloat16), centre, preferred_element_type=jnp.float32)
    return field + 2.0 * step_size * jnp.tanh(mixed + bias)


def flip_of(position):
    group = lax.div(position, GROUP)
    other_x = lax.bitwise_and(lax.bitwise_xor(group, lax.div(group, 4)), 1)
    return lax.bitwise_or(4 * other_x, lax.bitwise_and(group, 1))


def centre_kernel(weights, biases, whole, landing, offsets, sems):
    channels = whole.shape[1]
    copy = pltpu.make_async_copy(
        weights.at[0, pl.ds(4 * channels, channels)], landing, sems.at[0]
    )
    offset_copy = pltpu.make_async_copy(biases, offsets, sems.at[1])
    copy.start()
    offset_copy.start()
    offset_copy.wait()
    whole[channels:] = jnp.broadcast_to(offsets[0:1], (PAD, channels))
    copy.wait()
    whole[:channels] = landing[...].astype(jnp.float32)


def guess_kernel(initial, weights, biases, guessed, columns):
    first = fine(initial[...], weights, biases, 0, columns)
    guessed[...] = fine(first, weights, biases, 1, columns)


def force_kernel(incoming, initial, weights, biases, packed, columns):
    position = lax.axis_index("layer")
    rows, channels = packed.shape[1:]
    begin = jnp.where(position == 0, initial[...], incoming[...])
    relaxed = fine(begin, weights, biases, 0, columns)
    after = fine(relaxed, weights, biases, 1, columns)
    forcing = after - coarse(
        begin, weights[0, 4 * channels : 5 * channels], biases[0:1]
    )
    flip = flip_of(position)
    for lane in range(GROUP):
        spot = lax.bitwise_xor(flip, lane)
        packed[spot] = forcing[lane * rows : (lane + 1) * rows]


def hold_kernel(*refs):
    del refs


def part_kernel(begin, whole, after, part):
    del after
    part[...] = whole[begin : begin + part.shape[0]]


def lower_kernel(begin, counts, *refs):
    centres, offsets = refs[-2:]
    channels = centres.shape[1]
    at = 0
    for n, count in enumerate(counts):
        spot = 0
        for ref in refs[at : at + count]:
            rows = min(ref.shape[0], channels - spot)
            centres[begin + n, spot : spot + rows] = ref[:rows].astype(jnp.bfloat16)
            spot += rows
        offsets[begin + n] = ref[rows:]
        at += count


def chain_kernel(turn, last, state, near, near_bias, far, far_bias, extras, *refs):
    starts, end = (refs[-1], None) if last else refs[-2:]
    rows = starts.shape[1]
    position = lax.axis_index("layer")
    mine = lax.rem(position, GROUP)

    def walk(order):
        if turn:
            current = state[...]
        else:
            current = state[pl.ds(pl.multiple_of(mine * rows, rows), rows)]
        for at in range(GROUP):
            starts[at] = current
            centres, offsets = order[at // 4]
            slot = lax.bitwise_and(lax.bitwise_xor(mine, at), 3)
            current = coarse(current, centres[slot], offsets[slot, 0:1]) + extras[at]
        if not last:
            end[...] = current

    first, second = (near, near_bias), (far, far_bias)
    here = lax.div(position, GROUP) == turn
    pl.when(here & (mine < 4))(lambda: walk((first, second)))
    pl.when(here & (mine >= 4))(lambda: walk((second, first)))


def finish_kernel(arrived, packed, weights, biases, states, columns, whole):
    position = lax.axis_index("layer")
    channels = arrived.shape[2]
    flip = flip_of(position)
    begin = jnp.concatenate([arrived[lax.bitwise_xor(flip, lane)] for lane in range(GROUP)], axis=0)
    forcing = jnp.concatenate(
        [packed[lax.bitwise_xor(flip, lane)] for lane in range(GROUP)], axis=0
    )
    solved = coarse(begin, weights[0, 4 * channels : 5 * channels], biases[0:1]) + forcing
    finished = fine(begin, weights, biases, 0, columns)
    for layer, value in ((1, solved), (0, finished)):
        for band in range(channels // LANES):
            across = slice(band * LANES, (band + 1) * LANES)
            whole[layer, band] = value[:, across]
            for image in range(IMAGES):
                for row in range(SIDE):
                    states[layer, image, row, :, across] = whole[
                        layer, band, pl.ds(row * SIDE * IMAGES + image, SIDE, stride=IMAGES), :
                    ]


def solution(mesh):
    blocks = mesh.shape["layer"]
    parts = mesh.shape["batch"]
    groups = blocks // GROUP
    both = ("layer", "batch")

    def route(step):
        pairs = []
        for block in range(blocks):
            for part in range(parts):
                there, other = step(block, part)
                pairs.append((block * parts + part, there * parts + other))
        return pairs

    def over(block, part):
        return block ^ 2, (part + ((block >> 1) & 1) - (block & 1)) % parts

    behind = route(over)
    beside = route(lambda block, part: (block ^ 4, part))
    twin = route(lambda block, part: (block ^ 1, part))

    def shards(images, weights, biases):
        channels = images.shape[-1]
        cells = IMAGES * SIDE * SIDE
        rows = cells // GROUP
        columns = pltpu.VMEM((cells, 9 * channels), jnp.bfloat16)
        conv = 2 * cells * 9 * channels * channels

        own = call(
            centre_kernel,
            pltpu.VMEM((channels + PAD, channels), jnp.float32),
            [pltpu.with_memory_space_constraint(each, pltpu.HBM) for each in (weights, biases)],
            scratch=[
                pltpu.VMEM((channels, channels), jnp.bfloat16),
                pltpu.VMEM(biases.shape, jnp.float32),
                pltpu.SemaphoreType.DMA((2,)),
            ],
            specs=[HBM, HBM],
        )
        beside_x = lax.ppermute(own, both, beside)
        behind_z = lax.ppermute(own, both, behind)

        initial = images.astype(jnp.float32).reshape(IMAGES, SIDE * SIDE, channels)
        initial = jnp.transpose(initial, (1, 0, 2)).reshape(cells, channels)
        guessed = call(
            guess_kernel, f32(cells, channels), (initial, weights, biases), [columns], flops=2 * conv
        )
        incoming = lax.ppermute(guessed, "layer", [(i, i + 1) for i in range(blocks - 1)])
        packed = call(
            force_kernel,
            f32(GROUP, rows, channels),
            (incoming, initial, weights, biases),
            [columns],
            flops=2 * conv,
        )
        teams = [[g * GROUP + i for i in range(GROUP)] for g in range(groups)]
        extras = lax.all_to_all(packed, "layer", 0, 0, axis_index_groups=teams)

        def hold(each, *after):
            return call(
                hold_kernel,
                f32(*each.shape),
                (each, *after),
                specs=[ANY] * (1 + len(after)),
                out_specs=ANY,
                aliases={0: 0},
            )

        def lowered(begin, slots, held=()):
            pieces = [each for slot in slots for each in slot]
            return call(
                functools.partial(lower_kernel, begin, [len(slot) for slot in slots]),
                (
                    pltpu.VMEM((4, channels, channels), jnp.bfloat16),
                    pltpu.VMEM((4, PAD, channels), jnp.float32),
                ),
                (*pieces, *held),
                aliases={len(pieces) + n: n for n in range(len(held))},
            )

        def part(whole, begin, end, after):
            return call(
                functools.partial(part_kernel, begin),
                pltpu.VMEM((end - begin, channels), jnp.float32),
                (whole, after),
                specs=[VMEM, ANY],
            )

        behind_z = hold(behind_z, packed)
        beside_x = hold(beside_x, packed)
        corner = [
            lax.ppermute(part(beside_x, 0, CUT, extras), both, behind),
            lax.ppermute(part(behind_z, CUT, channels + PAD, extras), both, beside),
        ]
        own_twin = lax.ppermute(own, both, twin)
        behind_twin = lax.ppermute(behind_z, both, twin)
        beside_twin = lax.ppermute(beside_x, both, twin)
        near = lowered(0, ([own], [own_twin], [behind_z], [behind_twin]))
        far = lowered(0, ([beside_x], [beside_twin]))
        corner = [hold(each, near[1]) for each in corner]
        corner_twin = [lax.ppermute(each, both, twin) for each in corner]
        far = lowered(2, (corner, corner_twin), far)

        state = [initial]
        starts = None
        for turn in range(groups):
            operands = (*state, *near, *far, extras)
            if turn:
                pairs = [
                    (
                        (turn - 1) * GROUP + (lane ^ FLIPS[turn - 1]),
                        turn * GROUP + (lane ^ FLIPS[turn]),
                    )
                    for lane in range(GROUP)
                ]
                state = [lax.ppermute(*state, "layer", pairs)]
                operands = (*state, *near, *far, extras, starts)
            last = turn == groups - 1
            starts, *state = call(
                functools.partial(chain_kernel, turn, last),
                [f32(GROUP, rows, channels)] + [f32(rows, channels)] * (not last),
                operands,
                aliases={6: 0} if turn else None,
            )

        arrived = lax.all_to_all(starts, "layer", 0, 0, axis_index_groups=teams)
        return call(
            finish_kernel,
            f32(2, IMAGES, SIDE, SIDE, channels),
            (arrived, packed, weights, biases),
            [columns, pltpu.VMEM((2, channels // LANES, cells, LANES), jnp.float32)],
            flops=conv,
        )

    return jax.shard_map(
        shards,
        mesh=mesh,
        in_specs=(P("batch", None, None, None), P("layer", None, None), P("layer", None)),
        out_specs=P("layer", "batch", None, None, None),
        check_vma=False,
    )
```

```python
import functools

import jax
import jax.numpy as jnp
from jax import lax
from jax.experimental import pallas as pl
from jax.experimental.pallas import tpu as pltpu
from jax.sharding import PartitionSpec as P

step_size = 0.25
GROUP = 8
PAD = 8
CUT = 352
FLIPS = (0, 5, 0, 5, 4, 1, 4, 1)
SIDE = 4
IMAGES = 8
LANES = 128
MIB = 1 << 20

VMEM = pl.BlockSpec(memory_space=pltpu.VMEM)
ANY = pl.BlockSpec(memory_space=pl.ANY)
HBM = pl.BlockSpec(memory_space=pltpu.HBM)


def call(kernel, out_shape, operands, scratch=(), limit=8, flops=0, aliases=None, specs=None, out_specs=None):
    single = not isinstance(out_shape, (tuple, list))
    results = (out_shape,) if single else out_shape
    return pl.pallas_call(
        kernel,
        out_shape=out_shape,
        in_specs=specs or [VMEM] * len(operands),
        out_specs=out_specs or (VMEM if single else [VMEM for _ in out_shape]),
        scratch_shapes=list(scratch),
        input_output_aliases=aliases or {},
        compiler_params=pltpu.CompilerParams(vmem_limit_bytes=limit * MIB),
        cost_estimate=pl.CostEstimate(flops=0, bytes_accessed=0, transcendentals=0),
    )(*operands)


def f32(*shape):
    return jax.ShapeDtypeStruct(shape, jnp.float32)


def spread(field, columns):
    channels = field.shape[-1]
    cells = [field[IMAGES * at : IMAGES * (at + 1)] for at in range(SIDE * SIDE)]
    nothing = jnp.zeros_like(cells[0])
    for tap in range(9):
        down, right = tap // 3 - 1, tap % 3 - 1
        pieces = []
        for row in range(SIDE):
            for col in range(SIDE):
                inside = 0 <= row + down < SIDE and 0 <= col + right < SIDE
                pieces.append(cells[(row + down) * SIDE + col + right] if inside else nothing)
        columns[:, tap * channels : (tap + 1) * channels] = jnp.concatenate(pieces, axis=0).astype(
            jnp.bfloat16
        )


def fine(field, weights, biases, layer, columns):
    spread(field, columns)
    mixed = jnp.dot(columns[...], weights[layer], preferred_element_type=jnp.float32)
    return field + step_size * jnp.tanh(mixed + biases[layer : layer + 1])


def coarse(field, centre, bias):
    mixed = jnp.dot(field.astype(jnp.bfloat16), centre, preferred_element_type=jnp.float32)
    return field + 2.0 * step_size * jnp.tanh(mixed + bias)


def flip_of(position):
    group = lax.div(position, GROUP)
    other_x = lax.bitwise_and(lax.bitwise_xor(group, lax.div(group, 4)), 1)
    return lax.bitwise_or(4 * other_x, lax.bitwise_and(group, 1))


def centre_kernel(weights, biases, whole, landing, offsets, sems):
    channels = whole.shape[1]
    copy = pltpu.make_async_copy(
        weights.at[0, pl.ds(4 * channels, channels)], landing, sems.at[0]
    )
    offset_copy = pltpu.make_async_copy(biases, offsets, sems.at[1])
    copy.start()
    offset_copy.start()
    offset_copy.wait()
    whole[channels:] = jnp.broadcast_to(offsets[0:1], (PAD, channels))
    copy.wait()
    whole[:channels] = landing[...].astype(jnp.float32)


def guess_kernel(initial, weights, biases, guessed, columns):
    first = fine(initial[...], weights, biases, 0, columns)
    guessed[...] = fine(first, weights, biases, 1, columns)


def force_kernel(incoming, initial, weights, biases, packed, columns):
    position = lax.axis_index("layer")
    rows, channels = packed.shape[1:]
    begin = jnp.where(position == 0, initial[...], incoming[...])
    relaxed = fine(begin, weights, biases, 0, columns)
    after = fine(relaxed, weights, biases, 1, columns)
    forcing = after - coarse(
        begin, weights[0, 4 * channels : 5 * channels], biases[0:1]
    )
    flip = flip_of(position)
    for lane in range(GROUP):
        spot = lax.bitwise_xor(flip, lane)
        packed[spot] = forcing[lane * rows : (lane + 1) * rows]


def hold_kernel(*refs):
    del refs


def part_kernel(begin, whole, after, part):
    del after
    part[...] = whole[begin : begin + part.shape[0]]


def lower_kernel(begin, counts, *refs):
    centres, offsets = refs[-2:]
    channels = centres.shape[1]
    at = 0
    for n, count in enumerate(counts):
        spot = 0
        for ref in refs[at : at + count]:
            rows = min(ref.shape[0], channels - spot)
            centres[begin + n, spot : spot + rows] = ref[:rows].astype(jnp.bfloat16)
            spot += rows
        offsets[begin + n] = ref[rows:]
        at += count


def chain_kernel(turn, last, state, near, near_bias, far, far_bias, extras, *refs):
    starts, end = (refs[-1], None) if last else refs[-2:]
    rows = starts.shape[1]
    position = lax.axis_index("layer")
    mine = lax.rem(position, GROUP)

    def walk(order):
        if turn:
            current = state[...]
        else:
            current = state[pl.ds(pl.multiple_of(mine * rows, rows), rows)]
        for at in range(GROUP):
            starts[at] = current
            centres, offsets = order[at // 4]
            slot = lax.bitwise_and(lax.bitwise_xor(mine, at), 3)
            current = coarse(current, centres[slot], offsets[slot, 0:1]) + extras[at]
        if not last:
            end[...] = current

    first, second = (near, near_bias), (far, far_bias)
    here = lax.div(position, GROUP) == turn
    pl.when(here & (mine < 4))(lambda: walk((first, second)))
    pl.when(here & (mine >= 4))(lambda: walk((second, first)))


def finish_kernel(arrived, packed, weights, biases, states, columns, whole):
    position = lax.axis_index("layer")
    channels = arrived.shape[2]
    flip = flip_of(position)
    begin = jnp.concatenate([arrived[lax.bitwise_xor(flip, lane)] for lane in range(GROUP)], axis=0)
    forcing = jnp.concatenate(
        [packed[lax.bitwise_xor(flip, lane)] for lane in range(GROUP)], axis=0
    )
    solved = coarse(begin, weights[0, 4 * channels : 5 * channels], biases[0:1]) + forcing
    finished = fine(begin, weights, biases, 0, columns)
    for layer, value in ((1, solved), (0, finished)):
        for band in range(channels // LANES):
            across = slice(band * LANES, (band + 1) * LANES)
            whole[layer, band] = value[:, across]
            for image in range(IMAGES):
                for row in range(SIDE):
                    states[layer, image, row, :, across] = whole[
                        layer, band, pl.ds(row * SIDE * IMAGES + image, SIDE, stride=IMAGES), :
                    ]


def solution(mesh):
    blocks = mesh.shape["layer"]
    parts = mesh.shape["batch"]
    groups = blocks // GROUP
    both = ("layer", "batch")

    def route(step):
        pairs = []
        for block in range(blocks):
            for part in range(parts):
                there, other = step(block, part)
                pairs.append((block * parts + part, there * parts + other))
        return pairs

    def over(block, part):
        return block ^ 2, (part + ((block >> 1) & 1) - (block & 1)) % parts

    behind = route(over)
    beside = route(lambda block, part: (block ^ 4, part))
    twin = route(lambda block, part: (block ^ 1, part))

    def shards(images, weights, biases):
        channels = images.shape[-1]
        cells = IMAGES * SIDE * SIDE
        rows = cells // GROUP
        columns = pltpu.VMEM((cells, 9 * channels), jnp.bfloat16)
        conv = 2 * cells * 9 * channels * channels

        own = call(
            centre_kernel,
            pltpu.VMEM((channels + PAD, channels), jnp.float32),
            [pltpu.with_memory_space_constraint(each, pltpu.HBM) for each in (weights, biases)],
            scratch=[
                pltpu.VMEM((channels, channels), jnp.bfloat16),
                pltpu.VMEM(biases.shape, jnp.float32),
                pltpu.SemaphoreType.DMA((2,)),
            ],
            specs=[HBM, HBM],
        )
        beside_x = lax.ppermute(own, both, beside)
        behind_z = lax.ppermute(own, both, behind)

        initial = images.astype(jnp.float32).reshape(IMAGES, SIDE * SIDE, channels)
        initial = jnp.transpose(initial, (1, 0, 2)).reshape(cells, channels)
        guessed = call(
            guess_kernel, f32(cells, channels), (initial, weights, biases), [columns], flops=2 * conv
        )
        incoming = lax.ppermute(guessed, "layer", [(i, i + 1) for i in range(blocks - 1)])
        packed = call(
            force_kernel,
            f32(GROUP, rows, channels),
            (incoming, initial, weights, biases),
            [columns],
            flops=2 * conv,
        )
        teams = [[g * GROUP + i for i in range(GROUP)] for g in range(groups)]
        extras = lax.all_to_all(packed, "layer", 0, 0, axis_index_groups=teams)

        def hold(each, *after):
            return call(
                hold_kernel,
                f32(*each.shape),
                (each, *after),
                specs=[ANY] * (1 + len(after)),
                out_specs=ANY,
                aliases={0: 0},
            )

        def lowered(begin, slots, held=()):
            pieces = [each for slot in slots for each in slot]
            return call(
                functools.partial(lower_kernel, begin, [len(slot) for slot in slots]),
                (
                    pltpu.VMEM((4, channels, channels), jnp.bfloat16),
                    pltpu.VMEM((4, PAD, channels), jnp.float32),
                ),
                (*pieces, *held),
                aliases={len(pieces) + n: n for n in range(len(held))},
            )

        def part(whole, begin, end, after):
            return call(
                functools.partial(part_kernel, begin),
                pltpu.VMEM((end - begin, channels), jnp.float32),
                (whole, after),
                specs=[VMEM, ANY],
            )

        behind_z = hold(behind_z, packed)
        beside_x = hold(beside_x, packed)
        held = hold(own, extras)
        corner = [
            lax.ppermute(part(beside_x, 0, CUT, extras), both, behind),
            lax.ppermute(part(behind_z, CUT, channels + PAD, extras), both, beside),
        ]
        own_twin = lax.ppermute(held, both, twin)
        behind_twin = lax.ppermute(behind_z, both, twin)
        beside_twin = lax.ppermute(beside_x, both, twin)
        near = lowered(0, ([held], [own_twin], [behind_z], [behind_twin]))
        far = lowered(0, ([beside_x], [beside_twin]))
        corner = [hold(each, near[1]) for each in corner]
        corner_twin = [lax.ppermute(each, both, twin) for each in corner]
        far = lowered(2, (corner, corner_twin), far)

        state = [initial]
        starts = None
        for turn in range(groups):
            operands = (*state, *near, *far, extras)
            if turn:
                pairs = [
                    (
                        (turn - 1) * GROUP + (lane ^ FLIPS[turn - 1]),
                        turn * GROUP + (lane ^ FLIPS[turn]),
                    )
                    for lane in range(GROUP)
                ]
                state = [lax.ppermute(*state, "layer", pairs)]
                operands = (*state, *near, *far, extras, starts)
            last = turn == groups - 1
            starts, *state = call(
                functools.partial(chain_kernel, turn, last),
                [f32(GROUP, rows, channels)] + [f32(rows, channels)] * (not last),
                operands,
                aliases={6: 0} if turn else None,
            )

        arrived = lax.all_to_all(starts, "layer", 0, 0, axis_index_groups=teams)
        return call(
            finish_kernel,
            f32(2, IMAGES, SIDE, SIDE, channels),
            (arrived, packed, weights, biases),
            [columns, pltpu.VMEM((2, channels // LANES, cells, LANES), jnp.float32)],
            flops=conv,
        )

    return jax.shard_map(
        shards,
        mesh=mesh,
        in_specs=(P("batch", None, None, None), P("layer", None, None), P("layer", None)),
        out_specs=P("layer", "batch", None, None, None),
        check_vma=False,
    )
```
